256 devices in a mesh: wide: 32 (over x, z_hi, core), narrow: 8 (over y, z_lo).
Axes of the slice: x: 4, y: 4, z: 8 (z_hi: 4, z_lo: 2; z = z_hi * 2 + z_lo), core: 2. Of those that a mesh axis runs over, the one named last changes fastest.
Arguments:
- acts: float32 [2048, 6144], P(None, 'narrow'), may hold values from -6 to 6
- grads: float32 [2048, 6144], P(None, 'wide'), may hold values from -0.375 to 0.375
- basis_in: float32 [6144, 6144], P('narrow', 'wide'), may hold values from -0.078125 to 0.078125
- basis_out: float32 [6144, 6144], P('wide', 'narrow'), may hold values from -0.078125 to 0.078125
Outputs:
- moments: float32 [6144, 6144], P('narrow', 'wide')
The draws below stay inside these ranges and needn't reach their ends.
All inputs are finite; a program needn't handle non-finite values.
Results may differ from the reference program's by a relative error of at most 0.00012.
Values sent between devices are 32-bit elements; how exact they have to be, the bound alone decides.
No kernel may reach another device: no remote copies, remote signals or barrier semaphores. Data moves between devices by JAX's collectives and lax.ppermute only.
A program may use at most 64 MiB of HBM per device.

```python
import jax
import jax.numpy as jnp
from jax import lax

D = 6144
TOK_IMG = 256
IMAGES = 8
ROWS = 2048


def block_levels(key, dims, shards, least, top_value):
    loudness, own = 1.0, jax.random.fold_in(key, 6)
    for dim, parts in shards:
        steps = jnp.exp(jax.random.uniform(jax.random.fold_in(own, dim), (parts,), jnp.float32, least / len(shards), top_value / len(shards)))
        loudness = loudness * jnp.repeat(steps, dims[dim] // parts).reshape([-1 if axis == dim else 1 for axis in range(len(dims))])
    return loudness


def noise(rng, shape, spread, reach, split=(), dtype=jnp.bfloat16):
    loudness = block_levels(rng, shape, split, -0.22, 0.18) if split else 1.0
    array = jax.random.normal(rng, shape, jnp.float32) * spread * loudness
    return jnp.minimum(jnp.maximum(array, -reach), reach).astype(dtype)


def setup_inputs(seed: int = 0) -> dict:
    keys = jax.random.split(jax.random.key(seed), 5)
    return {
        "acts": noise(keys[0], (ROWS, D), 1.0, 6.0, ((1, 8),), jnp.float32),
        "grads": noise(keys[1], (ROWS, D), 0.0625, 0.375, ((1, 32),), jnp.float32),
        "basis_in": noise(keys[2], (D, D), D ** -0.5, 0.078125, ((0, 8), (1, 32)), jnp.float32),
        "basis_out": noise(keys[3], (D, D), D ** -0.5, 0.078125, ((0, 32), (1, 8)), jnp.float32),
    }


def reference(acts, grads, basis_in, basis_out):
    highest = lax.Precision.HIGHEST
    rotated_in = jnp.dot(acts, basis_in, precision=highest, preferred_element_type=jnp.float32)
    rotated_out = jnp.dot(grads, basis_out, precision=highest, preferred_element_type=jnp.float32)
    blocks_in = rotated_in.reshape(IMAGES, TOK_IMG, D)
    blocks_out = rotated_out.reshape(IMAGES, TOK_IMG, D)

    def accumulate(running, blocks):
        product_tile = jnp.dot(blocks[0].T, blocks[1], precision=highest, preferred_element_type=jnp.float32)
        return running + product_tile * product_tile, None

    running, _ = lax.scan(accumulate, jnp.zeros((D, D), jnp.float32), (blocks_out, blocks_in))
    return running / IMAGES
```

```python
import functools

import jax
import jax.numpy as jnp
from jax import lax
from jax.experimental import pallas as pl
from jax.experimental.pallas import tpu as pltpu
from jax.sharding import Mesh, PartitionSpec as P

IMAGES = 8
TOK = 256
HALF, QUARTER, PIECE = 128, 64, 16
VMEM_LIMIT = 48 * 1024 * 1024

EVEN = [(0, 1), (1, 0), (2, 3), (3, 2)]
ODD = [(0, 3), (3, 0), (1, 2), (2, 1)]
SWAP = [(0, 1), (1, 0)]


def ring(k):
    return [(i, (i + k) % 4) for i in range(4)]


def split(a):
    hi = a.astype(jnp.bfloat16)
    return hi, (a - hi.astype(jnp.float32)).astype(jnp.bfloat16)


def dot3(a, b, dims):
    a_hi, a_lo = split(a)
    b_hi, b_lo = split(b)
    dot = functools.partial(
        lax.dot_general, dimension_numbers=(dims, ((), ())), preferred_element_type=jnp.float32
    )
    return dot(a_hi, b_hi) + (dot(a_hi, b_lo) + dot(a_lo, b_hi))


def place(half, quarter, zh, at):
    row = (half ^ (at // 8)) * HALF + (quarter ^ (at // 4 % 2)) * QUARTER + ((zh + at % 4) % 4) * PIECE
    return pl.multiple_of(row, PIECE)


def out_kernel(flip, pos, g_own, g_other, b_own, b_other, keep, send, whole):
    h, b, zh = pos[1], pos[2], pos[3]
    half, quarter = (b, h) if flip else (h, b)
    g = jnp.concatenate([g_own[...], g_other[...]], axis=0).T
    basis = jnp.concatenate([b_own[...], b_other[...]], axis=0)
    whole[...] = dot3(g, basis, ((1,), (0,)))
    for at in range(16):
        to = keep if at < 8 else send
        to[pl.ds(at % 8 * PIECE, PIECE), :] = whole[pl.ds(place(half, quarter, zh, at), PIECE), :]


def rotate_out(pos, image, g_own, g_other, b_own, b_other):
    feat, cols = b_own.shape
    spec = lambda: pl.BlockSpec((feat, cols), lambda i, pos: (0, 0))
    out = lambda: pl.BlockSpec((HALF, cols), lambda i, pos: (0, 0))
    return pl.pallas_call(
        functools.partial(out_kernel, image % 2 == 1),
        grid_spec=pltpu.PrefetchScalarGridSpec(
            num_scalar_prefetch=1,
            grid=(1,),
            in_specs=[
                pl.BlockSpec((feat, TOK), lambda i, pos: (0, pos[0] * 4 + image)),
                pl.BlockSpec((feat, TOK), lambda i, pos: (0, image)),
                spec(),
                spec(),
            ],
            out_specs=[out(), out()],
            scratch_shapes=[pltpu.VMEM((TOK, cols), jnp.float32)],
        ),
        out_shape=[jax.ShapeDtypeStruct((HALF, cols), jnp.float32)] * 2,
        compiler_params=pltpu.CompilerParams(vmem_limit_bytes=VMEM_LIMIT),
        cost_estimate=pl.CostEstimate(flops=6 * TOK * 2 * feat * cols, bytes_accessed=4000000, transcendentals=0),
    )(pos, g_own, g_other, b_own, b_other)


def in_kernel(pos, acts, b_own, b_other, o0, o1, o2, o3, whole):
    y = pos[4]
    basis = jnp.concatenate([b_own[...], b_other[...]], axis=0)
    whole[...] = dot3(acts[...], basis, ((1,), (1,)))
    for k, to in enumerate((o0, o1, o2, o3)):
        to[...] = whole[pl.ds(pl.multiple_of((y + k) % 4 * QUARTER, QUARTER), QUARTER), :]


def rotate_in(pos, acts, b_own, b_other):
    cols, feat = b_own.shape
    spec = lambda: pl.BlockSpec((cols, feat), lambda i, pos: (0, 0))
    return pl.pallas_call(
        in_kernel,
        grid_spec=pltpu.PrefetchScalarGridSpec(
            num_scalar_prefetch=1,
            grid=(4,),
            in_specs=[pl.BlockSpec((TOK, feat), lambda i, pos: (pos[0] * 4 + i, 0)), spec(), spec()],
            out_specs=[pl.BlockSpec((QUARTER, 2 * cols), lambda i, pos: (i, 0)) for _ in range(4)],
            scratch_shapes=[pltpu.VMEM((TOK, 2 * cols), jnp.float32)],
        ),
        out_shape=[jax.ShapeDtypeStruct((4 * QUARTER, 2 * cols), jnp.float32)] * 4,
        compiler_params=pltpu.CompilerParams(vmem_limit_bytes=VMEM_LIMIT),
        cost_estimate=pl.CostEstimate(flops=24 * TOK * 2 * feat * cols, bytes_accessed=6000000, transcendentals=0),
    )(pos, acts, b_own, b_other)


def tile_kernel(first, pos, w_a, v_a, w_b, v_b, q0, q1, q2, q3, *rest):
    if first:
        own, other, left, right = rest
    else:
        own_in, other_in, own, other, left, right = rest
    h, b, zh, y = pos[1], pos[2], pos[3], pos[4]
    total = None
    for image, (w, v) in enumerate(((w_a, v_a), (w_b, v_b))):
        half, quarter = (b, h) if image else (h, b)
        for at in range(16):
            src = w if at < 8 else v
            right[pl.ds(place(half, quarter, zh, at), PIECE), :] = src[pl.ds(at % 8 * PIECE, PIECE), :]
        for k, q in enumerate((q0, q1, q2, q3)):
            left[pl.ds(pl.multiple_of((y + k) % 4 * QUARTER, QUARTER), QUARTER), :] = q[
                pl.ds(image * QUARTER, QUARTER), :
            ]
        tile = dot3(left[...].T, right[...], ((1,), (0,)))
        total = tile * tile if total is None else total + tile * tile
    cols = own.shape[0]
    if first:
        own[...] = total[:cols]
        other[...] = total[cols:]
    else:
        own[...] = own_in[...] + total[:cols]
        other[...] = other_in[...] + total[cols:]


def tiles(pos, pair, halves, quarters, running):
    rows, cols = halves[0].shape[1], quarters[0].shape[1] // 2
    full = lambda shape: pl.BlockSpec(shape, lambda i, pos: (0, 0))
    first = running is None
    return pl.pallas_call(
        functools.partial(tile_kernel, first),
        grid_spec=pltpu.PrefetchScalarGridSpec(
            num_scalar_prefetch=1,
            grid=(1,),
            in_specs=[full((HALF, rows))] * 4
            + [pl.BlockSpec((2 * QUARTER, 2 * cols), lambda i, pos: (pair, 0))] * 4
            + ([] if first else [full((cols, rows))] * 2),
            out_specs=[full((cols, rows))] * 2,
            scratch_shapes=[pltpu.VMEM((TOK, 2 * cols), jnp.float32), pltpu.VMEM((TOK, rows), jnp.float32)],
        ),
        out_shape=[jax.ShapeDtypeStruct((cols, rows), jnp.float32)] * 2,
        compiler_params=pltpu.CompilerParams(vmem_limit_bytes=VMEM_LIMIT),
        cost_estimate=pl.CostEstimate(flops=24 * TOK * rows * cols, bytes_accessed=6000000, transcendentals=0),
    )(pos, *halves, *quarters, *(() if first else running))


def local(acts, grads, basis_in, basis_out):
    send = lax.ppermute
    x, zh, c, y = (lax.axis_index(a) for a in ("x", "zh", "c", "y"))
    h = ((x == 1) | (x == 2)).astype(jnp.int32)
    b = (x >= 2).astype(jnp.int32)
    pos = jnp.stack([c.astype(jnp.int32), h, b, zh.astype(jnp.int32), y.astype(jnp.int32)])

    grads_t, basis_in_t = grads.T, basis_in.T
    rows = grads.shape[0] // 2
    theirs = lax.dynamic_slice(grads_t, (0, (1 - c) * rows), (grads_t.shape[0], rows))
    grads_other = send(theirs, "c", SWAP)
    basis_out_other = send(basis_out, "c", SWAP)
    basis_in_other = send(basis_in_t, "c", SWAP)

    done = []
    for pair in range(2):
        steps = (EVEN, ODD), (ODD, EVEN)
        sums = []
        for image, (near, far) in zip((2 * pair, 2 * pair + 1), steps):
            keep, give = rotate_out(pos, image, grads_t, grads_other, basis_out, basis_out_other)
            s = keep + send(give, "x", near)
            s = s[:QUARTER] + send(s[QUARTER:], "x", far)
            sums.append(s)
        pieces = [
            jnp.concatenate([s[k * PIECE : (k + 1) * PIECE] for s in sums], axis=0) for k in range(4)
        ]
        total = pieces[0]
        for k in (1, 3, 2):
            total = total + send(pieces[k], "zh", ring(k))
        back = [total] + [send(total, "zh", ring(-k)) for k in (1, 2, 3)]
        halves = []
        for image, (near, far) in enumerate(steps):
            mine = jnp.concatenate([p[image * PIECE : (image + 1) * PIECE] for p in back], axis=0)
            w = jnp.concatenate([mine, send(mine, "x", far)], axis=0)
            halves += [w, send(w, "x", near)]
        done.append(halves)

    parts = rotate_in(pos, acts, basis_in_t, basis_in_other)
    total = parts[0]
    for k in (1, 3, 2):
        total = total + send(parts[k], "y", ring(k))
    total = total + send(total, "zl", SWAP)
    quarters = [total] + [send(total, "y", ring(-k)) for k in (1, 2, 3)]

    running = None
    for pair in range(2):
        running = tiles(pos, pair, done[pair], quarters, running)
    own, other = running
    return ((own + send(other, "c", SWAP)) * (1.0 / IMAGES)).T


def solution(mesh):
    axes = Mesh(mesh.devices.reshape(4, 4, 2, 4, 2), ("x", "zh", "c", "y", "zl"))
    wide, narrow = ("x", "zh", "c"), ("y", "zl")
    placed = (P(None, narrow), P(None, wide), P(narrow, wide), P(wide, narrow))
    return jax.shard_map(
        local, mesh=axes, in_specs=placed, out_specs=P(narrow, wide), check_vma=False
    )
```

```python
import functools

import jax
import jax.numpy as jnp
from jax import lax
from jax.experimental import pallas as pl
from jax.experimental.pallas import tpu as pltpu
from jax.sharding import Mesh, PartitionSpec as P

IMAGES = 8
TOK = 256
PIECE = 16
VMEM_LIMIT = 48 * 1024 * 1024
SWAP = [(0, 1), (1, 0)]

CHUNKS = (((0, 1), True), ((2, 3), True))


def partner(i, bit):
    return i ^ 1 if bit else 3 - i


def swap_pairs(step, index):
    return [
        (index(i, c), index(partner(i, (step + c) % 2 == 0), c)) for i in range(4) for c in range(2)
    ]


def split(a):
    hi = a.astype(jnp.bfloat16)
    return hi, (a - hi.astype(jnp.float32)).astype(jnp.bfloat16)


def dot3(a, b, dims):
    a_hi, a_lo = split(a)
    b_hi, b_lo = split(b)
    dot = functools.partial(
        lax.dot_general, dimension_numbers=(dims, ((), ())), preferred_element_type=jnp.float32
    )
    return dot(a_hi, b_hi) + (dot(a_hi, b_lo) + dot(a_lo, b_hi))


def row(at, own, size):
    return pl.multiple_of((own ^ at) * size, size)


def out_kernel(x_first, pos, g_own, g_other, b_own, b_other, keep, send, whole):
    own = pos[1 if x_first else 2]
    g = jnp.concatenate([g_own[...], g_other[...]], axis=0).T
    basis = jnp.concatenate([b_own[...], b_other[...]], axis=0)
    whole[...] = dot3(g, basis, ((1,), (0,)))
    for at in range(16):
        to = keep if at < 8 else send
        to[0, pl.ds(at % 8 * PIECE, PIECE), :] = whole[pl.ds(row(at, own, PIECE), PIECE), :]


def rotate_out(pos, chunk, g_own, g_other, b_own, b_other):
    (images, x_first), (feat, cols) = chunk, b_own.shape
    n, first = len(images), images[0]
    spec = lambda: pl.BlockSpec((feat, cols), lambda i, pos: (0, 0))
    return pl.pallas_call(
        functools.partial(out_kernel, x_first),
        grid_spec=pltpu.PrefetchScalarGridSpec(
            num_scalar_prefetch=1,
            grid=(n,),
            in_specs=[
                pl.BlockSpec((feat, TOK), lambda i, pos: (0, pos[0] * 4 + first + i)),
                pl.BlockSpec((feat, TOK), lambda i, pos: (0, first + i)),
                spec(),
                spec(),
            ],
            out_specs=[pl.BlockSpec((1, TOK // 2, cols), lambda i, pos: (i, 0, 0))] * 2,
            scratch_shapes=[pltpu.VMEM((TOK, cols), jnp.float32)],
        ),
        out_shape=[jax.ShapeDtypeStruct((n, TOK // 2, cols), jnp.float32)] * 2,
        compiler_params=pltpu.CompilerParams(vmem_limit_bytes=VMEM_LIMIT),
        cost_estimate=pl.CostEstimate(
            flops=6 * n * TOK * 2 * feat * cols, bytes_accessed=4000000, transcendentals=0
        ),
    )(pos, g_own, g_other, b_own, b_other)


def in_kernel(pos, acts, b_own, b_other, keep, send, whole):
    own = pos[3]
    basis = jnp.concatenate([b_own[...], b_other[...]], axis=0)
    whole[...] = dot3(acts[...], basis, ((1,), (1,)))
    size = TOK // 4
    for at in range(4):
        to = keep if at < 2 else send
        to[0, pl.ds(at % 2 * size, size), :] = whole[pl.ds(row(at, own, size), size), :]


def rotate_in(pos, acts, b_own, b_other):
    cols, feat = b_own.shape
    spec = lambda: pl.BlockSpec((cols, feat), lambda i, pos: (0, 0))
    return pl.pallas_call(
        in_kernel,
        grid_spec=pltpu.PrefetchScalarGridSpec(
            num_scalar_prefetch=1,
            grid=(4,),
            in_specs=[pl.BlockSpec((TOK, feat), lambda i, pos: (pos[0] * 4 + i, 0)), spec(), spec()],
            out_specs=[pl.BlockSpec((1, TOK // 2, 2 * cols), lambda i, pos: (i, 0, 0))] * 2,
            scratch_shapes=[pltpu.VMEM((TOK, 2 * cols), jnp.float32)],
        ),
        out_shape=[jax.ShapeDtypeStruct((4, TOK // 2, 2 * cols), jnp.float32)] * 2,
        compiler_params=pltpu.CompilerParams(vmem_limit_bytes=VMEM_LIMIT),
        cost_estimate=pl.CostEstimate(flops=24 * TOK * 2 * feat * cols, bytes_accessed=6000000, transcendentals=0),
    )(pos, acts, b_own, b_other)


def tile_kernel(chunk, first, pos, w, v, q, p, *rest):
    images, x_first = chunk
    if first:
        own, other, left, right = rest
    else:
        own_in, other_in, own, other, left, right = rest
    own_out, own_y = pos[1 if x_first else 2], pos[3]
    size = TOK // 4
    total = None
    for i, image in enumerate(images):
        for at in range(16):
            src = w if at < 8 else v
            right[pl.ds(row(at, own_out, PIECE), PIECE), :] = src[i, pl.ds(at % 8 * PIECE, PIECE), :]
        for at in range(4):
            src = q if at < 2 else p
            left[pl.ds(row(at, own_y, size), size), :] = src[image, pl.ds(at % 2 * size, size), :]
        tile = dot3(left[...].T, right[...], ((1,), (0,)))
        total = tile * tile if total is None else total + tile * tile
    cols = own.shape[0]
    if first:
        own[...] = total[:cols]
        other[...] = total[cols:]
    else:
        own[...] = own_in[...] + total[:cols]
        other[...] = other_in[...] + total[cols:]


def tiles(pos, chunk, halves, quarters, running):
    rows, cols = halves[0].shape[2], quarters[0].shape[2] // 2
    full = lambda a: pl.BlockSpec(a.shape, lambda i, pos: (0,) * a.ndim)
    first = running is None
    args = (*halves, *quarters, *(() if first else running))
    out = jax.ShapeDtypeStruct((cols, rows), jnp.float32)
    return pl.pallas_call(
        functools.partial(tile_kernel, chunk, first),
        grid_spec=pltpu.PrefetchScalarGridSpec(
            num_scalar_prefetch=1,
            grid=(1,),
            in_specs=[full(a) for a in args],
            out_specs=[full(out)] * 2,
            scratch_shapes=[pltpu.VMEM((TOK, 2 * cols), jnp.float32), pltpu.VMEM((TOK, rows), jnp.float32)],
        ),
        out_shape=[out] * 2,
        compiler_params=pltpu.CompilerParams(vmem_limit_bytes=VMEM_LIMIT),
        cost_estimate=pl.CostEstimate(
            flops=12 * len(chunk[0]) * TOK * rows * cols, bytes_accessed=6000000, transcendentals=0
        ),
    )(pos, *args)


def exchange(a, axis, step):
    if axis == "y":
        return lax.ppermute(a, ("c", "y"), swap_pairs(step, lambda i, c: 4 * c + i))
    return lax.ppermute(a, (axis, "c"), swap_pairs(step, lambda i, c: 2 * i + c))


def reduced(keep, give, steps):
    for i, (axis, step) in enumerate(steps):
        got = exchange(give, axis, step)
        if i + 1 == len(steps):
            return keep + got
        half = keep.shape[1] // 2
        keep, give = keep[:, :half] + got[:, :half], keep[:, half:] + got[:, half:]


def gathered(a, steps):
    for i, (axis, step) in enumerate(reversed(steps)):
        got = exchange(a, axis, step)
        if i + 1 == len(steps):
            return a, got
        a = jnp.concatenate([a, got], axis=1)


def local(acts, grads, basis_in, basis_out):
    x, zh, c, y = (lax.axis_index(a).astype(jnp.int32) for a in ("x", "zh", "c", "y"))

    def bits(i):
        near, far = ((i == 1) | (i == 2)).astype(jnp.int32), (i >= 2).astype(jnp.int32)
        return jnp.where(c == 0, 2 * near + far, 2 * far + near)

    pos = jnp.stack([c, 4 * bits(x) + bits(zh), 4 * bits(zh) + bits(x), bits(y)])

    grads_t, basis_in_t = grads.T, basis_in.T
    rows = grads.shape[0] // 2
    basis_out_other = lax.ppermute(basis_out, "c", SWAP)
    theirs = lax.dynamic_slice(grads_t, (0, (1 - c) * rows), (grads_t.shape[0], rows))
    grads_other = lax.ppermute(theirs, "c", SWAP)
    basis_in_t, _ = lax.optimization_barrier((basis_in_t, grads_other))
    basis_in_other = lax.ppermute(basis_in_t, "c", SWAP)

    along_x, along_z = (("x", 0), ("x", 1)), (("zh", 0), ("zh", 1))
    whole = []
    for chunk in CHUNKS:
        steps = along_x + along_z if chunk[1] else along_z + along_x
        keep, give = rotate_out(pos, chunk, grads_t, grads_other, basis_out, basis_out_other)
        whole.append(gathered(reduced(keep, give, steps), steps))

    along_y = (("y", 0), ("y", 1))
    keep, give = rotate_in(pos, acts, basis_in_t, basis_in_other)
    total = reduced(keep, give, along_y)
    total = total + lax.ppermute(total, "zl", SWAP)
    quarters = gathered(total, along_y)

    running = None
    for chunk, halves in zip(CHUNKS, whole):
        running = tiles(pos, chunk, halves, quarters, running)
    own, other = running
    return ((own + lax.ppermute(other, "c", SWAP)) * (1.0 / IMAGES)).T


def solution(mesh):
    axes = Mesh(mesh.devices.reshape(4, 4, 2, 4, 2), ("x", "zh", "c", "y", "zl"))
    wide, narrow = ("x", "zh", "c"), ("y", "zl")
    placed = (P(None, narrow), P(None, wide), P(narrow, wide), P(wide, narrow))
    return jax.shard_map(
        local, mesh=axes, in_specs=placed, out_specs=P(narrow, wide), check_vma=False
    )
```

```python
import functools

import jax
import jax.numpy as jnp
from jax import lax
from jax.experimental import pallas as pl
from jax.experimental.pallas import tpu as pltpu
from jax.sharding import Mesh, PartitionSpec as P

IMAGES = 8
TOK = 256
PIECE = 32
VMEM_LIMIT = 28 * 1024 * 1024
SWAP = [(0, 1), (1, 0)]
FREE = pl.CostEstimate(flops=0, bytes_accessed=0, transcendentals=0)

CHUNKS = (((0, 1), True), ((2, 3), True))


def partner(i, bit):
    return i ^ 1 if bit else 3 - i


def swap_pairs(step, index):
    return [
        (index(i, c), index(partner(i, (step + c) % 2 == 0), c)) for i in range(4) for c in range(2)
    ]


def split(a):
    hi = a.astype(jnp.bfloat16)
    return hi, (a - hi.astype(jnp.float32)).astype(jnp.bfloat16)


def dot3(a, b, dims):
    a_hi, a_lo = split(a)
    b_hi, b_lo = split(b)
    dot = functools.partial(
        lax.dot_general, dimension_numbers=(dims, ((), ())), preferred_element_type=jnp.float32
    )
    return dot(a_hi, b_hi) + (dot(a_hi, b_lo) + dot(a_lo, b_hi))


def bits(i, c):
    return (i + 1) // 2 % 2 * (2 - c) + i // 2 * (1 + c)


def own_piece(pos, x_first):
    x, zh = bits(pos[1], pos[0]), bits(pos[2], pos[0])
    return 2 * x + zh // 2 if x_first else 2 * zh + x // 2


def row(at, own, size):
    return pl.multiple_of((own ^ at) * size, size)


def out_kernel(x_first, pos, g_own, g_other, b_own, b_other, keep, send, whole):
    own = own_piece(pos, x_first)
    g = jnp.concatenate([g_own[...], g_other[...]], axis=0).T
    basis = jnp.concatenate([b_own[...], b_other[...]], axis=0)
    whole[...] = dot3(g, basis, ((1,), (0,)))
    for at in range(8):
        to = keep if at < 4 else send
        to[0, pl.ds(at % 4 * PIECE, PIECE), :] = whole[pl.ds(row(at, own, PIECE), PIECE), :]


def rotate_out(pos, chunk, base, g_own, g_other, b_own, b_other):
    (images, x_first), (feat, cols) = chunk, b_own.shape
    n, first = len(images), images[0] - base
    spec = lambda: pl.BlockSpec((feat, cols), lambda i, pos: (0, 0))
    return pl.pallas_call(
        functools.partial(out_kernel, x_first),
        grid_spec=pltpu.PrefetchScalarGridSpec(
            num_scalar_prefetch=1,
            grid=(n,),
            in_specs=[
                pl.BlockSpec((feat, TOK), lambda i, pos: (0, first + i)),
                pl.BlockSpec((feat, TOK), lambda i, pos: (0, first + i)),
                spec(),
                spec(),
            ],
            out_specs=[pl.BlockSpec((1, TOK // 2, cols), lambda i, pos: (i, 0, 0))] * 2,
            scratch_shapes=[pltpu.VMEM((TOK, cols), jnp.float32)],
        ),
        out_shape=[jax.ShapeDtypeStruct((n, TOK // 2, cols), jnp.float32)] * 2,
        compiler_params=pltpu.CompilerParams(vmem_limit_bytes=VMEM_LIMIT),
        cost_estimate=FREE,
    )(pos, g_own, g_other, b_own, b_other)


def in_kernel(pos, acts, b_own, b_other, keep, send, whole):
    own = bits(pos[3], pos[0])
    basis = jnp.concatenate([b_own[...], b_other[...]], axis=0)
    whole[...] = dot3(acts[...], basis, ((1,), (1,)))
    size = TOK // 4
    for at in range(4):
        to = keep if at < 2 else send
        to[0, pl.ds(at % 2 * size, size), :] = whole[pl.ds(row(at, own, size), size), :]


def rotate_in(pos, acts, b_own, b_other):
    cols, feat = b_own.shape
    spec = lambda: pl.BlockSpec((cols, feat), lambda i, pos: (0, 0))
    return pl.pallas_call(
        in_kernel,
        grid_spec=pltpu.PrefetchScalarGridSpec(
            num_scalar_prefetch=1,
            grid=(4,),
            in_specs=[pl.BlockSpec((TOK, feat), lambda i, pos: (pos[0] * 4 + i, 0)), spec(), spec()],
            out_specs=[pl.BlockSpec((1, TOK // 2, 2 * cols), lambda i, pos: (i, 0, 0))] * 2,
            scratch_shapes=[pltpu.VMEM((TOK, 2 * cols), jnp.float32)],
        ),
        out_shape=[jax.ShapeDtypeStruct((4, TOK // 2, 2 * cols), jnp.float32)] * 2,
        compiler_params=pltpu.CompilerParams(vmem_limit_bytes=VMEM_LIMIT),
        cost_estimate=FREE,
    )(pos, acts, b_own, b_other)


def tile_kernel(chunk, first, pos, w, v, q, p, *rest):
    images, x_first = chunk
    if first:
        own, other, left, right = rest
    else:
        own_in, other_in, own, other, left, right = rest
    own_out, own_y = own_piece(pos, x_first), bits(pos[3], pos[0])
    size = TOK // 4
    total = None
    for i, image in enumerate(images):
        for at in range(8):
            src = w if at < 4 else v
            right[pl.ds(row(at, own_out, PIECE), PIECE), :] = src[i, pl.ds(at % 4 * PIECE, PIECE), :]
        for at in range(4):
            src = q if at < 2 else p
            left[pl.ds(row(at, own_y, size), size), :] = src[image, pl.ds(at % 2 * size, size), :]
        tile = dot3(left[...].T, right[...], ((1,), (0,)))
        total = tile * tile if total is None else total + tile * tile
    cols = own.shape[0]
    if first:
        own[...] = total[:cols]
        other[...] = total[cols:]
    else:
        own[...] = own_in[...] + total[:cols]
        other[...] = other_in[...] + total[cols:]


def tiles(pos, chunk, halves, quarters, running):
    rows, cols = halves[0].shape[2], quarters[0].shape[2] // 2
    full = lambda a: pl.BlockSpec(a.shape, lambda i, pos: (0,) * a.ndim)
    first = running is None
    args = (*halves, *quarters, *(() if first else running))
    out = jax.ShapeDtypeStruct((cols, rows), jnp.float32)
    return pl.pallas_call(
        functools.partial(tile_kernel, chunk, first),
        grid_spec=pltpu.PrefetchScalarGridSpec(
            num_scalar_prefetch=1,
            grid=(1,),
            in_specs=[full(a) for a in args],
            out_specs=[full(out)] * 2,
            scratch_shapes=[pltpu.VMEM((TOK, 2 * cols), jnp.float32), pltpu.VMEM((TOK, rows), jnp.float32)],
        ),
        out_shape=[out] * 2,
        compiler_params=pltpu.CompilerParams(vmem_limit_bytes=VMEM_LIMIT),
        cost_estimate=FREE,
    )(pos, *args)


def exchange(a, axis, step):
    if axis == "zl":
        return lax.ppermute(a, axis, SWAP)
    if axis == "y":
        return lax.ppermute(a, ("c", "y"), swap_pairs(step, lambda i, c: 4 * c + i))
    return lax.ppermute(a, (axis, "c"), swap_pairs(step, lambda i, c: 2 * i + c))


def after(value, other):
    return value if other is None else lax.optimization_barrier((value, other))[0]


def travel(parts, steps, inner):
    keep, give = parts
    for i, (axis, step) in enumerate(steps):
        got = yield give, axis, step
        if i + 1 == len(steps):
            keep = keep + got
        else:
            half = keep.shape[1] // 2
            keep, give = keep[:, :half] + got[:, :half], keep[:, half:] + got[:, half:]
    keep = keep + (yield keep, *inner)
    for i, (axis, step) in enumerate(reversed(steps)):
        got = yield keep, axis, step
        if i + 1 < len(steps):
            keep = jnp.concatenate([keep, got], axis=1)
    yield keep, got


def local(acts, grads, basis_in, basis_out):
    x, zh, c, y = (lax.axis_index(a).astype(jnp.int32) for a in ("x", "zh", "c", "y"))

    pos = jnp.stack([c, x, zh, y])
    grads_t, basis_in_t = grads.T, basis_in.T

    to_other = lambda a: lax.ppermute(a, "c", SWAP)
    basis_out_other = to_other(basis_out)
    feat, ahead = grads_t.shape[0], len(CHUNKS[0][0])

    def swapped(first, count, token):
        columns = lambda core: lax.dynamic_slice(
            after(grads_t, token), (0, (core * 4 + first) * TOK), (feat, count * TOK)
        )
        return columns(c), to_other(columns(1 - c))

    grads_of = {0: (0, *swapped(0, ahead, None))}

    def output_side(i, token):
        images, x_first = chunk = CHUNKS[i]
        along = [[("x", 0), ("x", 1)], [("zh", 0), ("zh", 1)]][:: 1 if x_first else -1]
        part = 0 if i == 0 else 1
        if part not in grads_of:
            grads_of[1] = (ahead, *swapped(ahead, 4 - ahead, token))
        parts = rotate_out(after(pos, token), chunk, *grads_of[part], basis_out, basis_out_other)
        return travel(parts, along[0] + along[1][:1], along[1][1])

    def input_side(token):
        own = after(basis_in_t, token)
        parts = rotate_in(pos, acts, own, to_other(own))
        return travel(parts, [("y", 0), ("y", 1)], ("zl", 0))

    last = len(CHUNKS)
    chains, flying, results, token = {}, {}, {}, None
    for i in range(last + 1):
        chains[i] = output_side(i, token) if i < last else input_side(token)
        out = next(chains[i])
        flying[i], token = exchange(*out), out[0]
    while len(results) <= last:
        for i in chains:
            if i in results:
                continue
            out = chains[i].send(flying[i])
            if len(out) == 2:
                results[i] = out
            else:
                flying[i] = exchange(*out)

    running = None
    for i in range(last):
        running = tiles(pos, CHUNKS[i], results[i], results[last], running)
    own, other = running
    return ((own + to_other(other)) * (1.0 / IMAGES)).T


def solution(mesh):
    axes = Mesh(mesh.devices.reshape(4, 4, 2, 4, 2), ("x", "zh", "c", "y", "zl"))
    wide, narrow = ("x", "zh", "c"), ("y", "zl")
    placed = (P(None, narrow), P(None, wide), P(narrow, wide), P(wide, narrow))
    return jax.shard_map(
        local, mesh=axes, in_specs=placed, out_specs=P(narrow, wide), check_vma=False
    )
```

```python
import functools

import jax
import jax.numpy as jnp
from jax import lax
from jax.experimental import pallas as pl
from jax.experimental.pallas import tpu as pltpu
from jax.sharding import Mesh, PartitionSpec as P

IMAGES = 8
TOK = 256
PIECE = 32
VMEM_LIMIT = 28 * 1024 * 1024
SWAP = [(0, 1), (1, 0)]
FREE = pl.CostEstimate(flops=0, bytes_accessed=0, transcendentals=0)

CHUNKS = (((0, 1), 'xxz'), ((2,), 'xxz'), ((3,), 'xzz'))


def partner(i, bit):
    return i ^ 1 if bit else 3 - i


def swap_pairs(step, index):
    return [
        (index(i, c), index(partner(i, (step + c) % 2 == 0), c)) for i in range(4) for c in range(2)
    ]


def split(a):
    hi = a.astype(jnp.bfloat16)
    return hi, (a - hi.astype(jnp.float32)).astype(jnp.bfloat16)


def dot3(a, b, dims):
    a_hi, a_lo = split(a)
    b_hi, b_lo = split(b)
    dot = functools.partial(
        lax.dot_general, dimension_numbers=(dims, ((), ())), preferred_element_type=jnp.float32
    )
    return dot(a_hi, b_hi) + (dot(a_hi, b_lo) + dot(a_lo, b_hi))


def bits(i, c):
    return (i + 1) // 2 % 2 * (2 - c) + i // 2 * (1 + c)


def own_piece(pos, order):
    x, zh = bits(pos[1], pos[0]), bits(pos[2], pos[0])
    return {"xxz": 2 * x + zh // 2, "xzz": x // 2 * 4 + zh, "zzx": 2 * zh + x // 2}[order]


def row(at, own, size):
    return pl.multiple_of((own ^ at) * size, size)


def out_kernel(order, pos, g_own, g_other, b_own, b_other, keep, send, whole):
    own = own_piece(pos, order)
    g = jnp.concatenate([g_own[...], g_other[...]], axis=0).T
    basis = jnp.concatenate([b_own[...], b_other[...]], axis=0)
    whole[...] = dot3(g, basis, ((1,), (0,)))
    for at in range(8):
        to = keep if at < 4 else send
        to[0, pl.ds(at % 4 * PIECE, PIECE), :] = whole[pl.ds(row(at, own, PIECE), PIECE), :]


def rotate_out(pos, chunk, base, g_own, g_other, b_own, b_other):
    (images, order), (feat, cols) = chunk, b_own.shape
    n, first = len(images), images[0] - base
    spec = lambda: pl.BlockSpec((feat, cols), lambda i, pos: (0, 0))
    return pl.pallas_call(
        functools.partial(out_kernel, order),
        grid_spec=pltpu.PrefetchScalarGridSpec(
            num_scalar_prefetch=1,
            grid=(n,),
            in_specs=[
                pl.BlockSpec((feat, TOK), lambda i, pos: (0, first + i)),
                pl.BlockSpec((feat, TOK), lambda i, pos: (0, first + i)),
                spec(),
                spec(),
            ],
            out_specs=[pl.BlockSpec((1, TOK // 2, cols), lambda i, pos: (i, 0, 0))] * 2,
            scratch_shapes=[pltpu.VMEM((TOK, cols), jnp.float32)],
        ),
        out_shape=[jax.ShapeDtypeStruct((n, TOK // 2, cols), jnp.float32)] * 2,
        compiler_params=pltpu.CompilerParams(vmem_limit_bytes=VMEM_LIMIT),
        cost_estimate=FREE,
    )(pos, g_own, g_other, b_own, b_other)


def in_kernel(pos, acts, b_own, b_other, keep, send, whole):
    own = bits(pos[3], pos[0])
    basis = jnp.concatenate([b_own[...], b_other[...]], axis=0)
    whole[...] = dot3(acts[...], basis, ((1,), (1,)))
    size = TOK // 4
    for at in range(4):
        to = keep if at < 2 else send
        to[0, pl.ds(at % 2 * size, size), :] = whole[pl.ds(row(at, own, size), size), :]


def rotate_in(pos, acts, b_own, b_other):
    cols, feat = b_own.shape
    spec = lambda: pl.BlockSpec((cols, feat), lambda i, pos: (0, 0))
    return pl.pallas_call(
        in_kernel,
        grid_spec=pltpu.PrefetchScalarGridSpec(
            num_scalar_prefetch=1,
            grid=(4,),
            in_specs=[pl.BlockSpec((TOK, feat), lambda i, pos: (pos[0] * 4 + i, 0)), spec(), spec()],
            out_specs=[pl.BlockSpec((1, TOK // 2, 2 * cols), lambda i, pos: (i, 0, 0))] * 2,
            scratch_shapes=[pltpu.VMEM((TOK, 2 * cols), jnp.float32)],
        ),
        out_shape=[jax.ShapeDtypeStruct((4, TOK // 2, 2 * cols), jnp.float32)] * 2,
        compiler_params=pltpu.CompilerParams(vmem_limit_bytes=VMEM_LIMIT),
        cost_estimate=FREE,
    )(pos, acts, b_own, b_other)


def tile_kernel(chunk, first, pos, w, v, q, p, *rest):
    images, order = chunk
    if first:
        own, other, left, right = rest
    else:
        own_in, other_in, own, other, left, right = rest
    own_out, own_y = own_piece(pos, order), bits(pos[3], pos[0])
    size = TOK // 4
    total = None
    for i, image in enumerate(images):
        for at in range(8):
            src = w if at < 4 else v
            right[pl.ds(row(at, own_out, PIECE), PIECE), :] = src[i, pl.ds(at % 4 * PIECE, PIECE), :]
        for at in range(4):
            src = q if at < 2 else p
            left[pl.ds(row(at, own_y, size), size), :] = src[image, pl.ds(at % 2 * size, size), :]
        tile = dot3(left[...].T, right[...], ((1,), (0,)))
        total = tile * tile if total is None else total + tile * tile
    cols = own.shape[0]
    if first:
        own[...] = total[:cols]
        other[...] = total[cols:]
    else:
        own[...] = own_in[...] + total[:cols]
        other[...] = other_in[...] + total[cols:]


def tiles(pos, chunk, halves, quarters, running):
    rows, cols = halves[0].shape[2], quarters[0].shape[2] // 2
    full = lambda a: pl.BlockSpec(a.shape, lambda i, pos: (0,) * a.ndim)
    first = running is None
    args = (*halves, *quarters, *(() if first else running))
    out = jax.ShapeDtypeStruct((cols, rows), jnp.float32)
    return pl.pallas_call(
        functools.partial(tile_kernel, chunk, first),
        grid_spec=pltpu.PrefetchScalarGridSpec(
            num_scalar_prefetch=1,
            grid=(1,),
            in_specs=[full(a) for a in args],
            out_specs=[full(out)] * 2,
            scratch_shapes=[pltpu.VMEM((TOK, 2 * cols), jnp.float32), pltpu.VMEM((TOK, rows), jnp.float32)],
        ),
        out_shape=[out] * 2,
        compiler_params=pltpu.CompilerParams(vmem_limit_bytes=VMEM_LIMIT),
        cost_estimate=FREE,
    )(pos, *args)


def exchange(a, axis, step):
    if axis == "zl":
        return lax.ppermute(a, axis, SWAP)
    if axis == "y":
        return lax.ppermute(a, ("c", "y"), swap_pairs(step, lambda i, c: 4 * c + i))
    return lax.ppermute(a, (axis, "c"), swap_pairs(step, lambda i, c: 2 * i + c))


def after(value, other):
    return value if other is None else lax.optimization_barrier((value, other))[0]


def travel(parts, steps, inner):
    keep, give = parts
    for i, (axis, step) in enumerate(steps):
        got = yield give, axis, step
        if i + 1 == len(steps):
            keep = keep + got
        else:
            half = keep.shape[1] // 2
            keep, give = keep[:, :half] + got[:, :half], keep[:, half:] + got[:, half:]
    keep = keep + (yield keep, *inner)
    for i, (axis, step) in enumerate(reversed(steps)):
        got = yield keep, axis, step
        if i + 1 < len(steps):
            keep = jnp.concatenate([keep, got], axis=1)
    yield keep, got


def local(acts, grads, basis_in, basis_out):
    x, zh, c, y = (lax.axis_index(a).astype(jnp.int32) for a in ("x", "zh", "c", "y"))

    pos = jnp.stack([c, x, zh, y])
    grads_t, basis_in_t = grads.T, basis_in.T

    to_other = lambda a: lax.ppermute(a, "c", SWAP)
    basis_out_other = to_other(basis_out)
    feat, ahead = grads_t.shape[0], len(CHUNKS[0][0])

    def swapped(first, count, token):
        columns = lambda core: lax.dynamic_slice(
            after(grads_t, token), (0, (core * 4 + first) * TOK), (feat, count * TOK)
        )
        return columns(c), to_other(columns(1 - c))

    grads_of = {0: (0, *swapped(0, ahead, None))}

    def output_side(i, token):
        images, order = chunk = CHUNKS[i]
        left = {"x": [("x", 0), ("x", 1)], "z": [("zh", 0), ("zh", 1)]}
        steps = [left[axis].pop(0) for axis in order]
        part = 0 if i == 0 else 1
        if part not in grads_of:
            grads_of[1] = (ahead, *swapped(ahead, 4 - ahead, token))
        parts = rotate_out(after(pos, token), chunk, *grads_of[part], basis_out, basis_out_other)
        return travel(parts, steps, (left["x"] + left["z"])[0])

    def input_side(token):
        own = after(basis_in_t, token)
        parts = rotate_in(pos, acts, own, to_other(own))
        return travel(parts, [("y", 0), ("y", 1)], ("zl", 0))

    last = len(CHUNKS)
    chains, flying, results, token = {}, {}, {}, None
    for i in range(last + 1):
        chains[i] = output_side(i, token) if i < last else input_side(token)
        out = next(chains[i])
        flying[i], token = exchange(*out), out[0]
    while len(results) <= last:
        for i in chains:
            if i in results:
                continue
            out = chains[i].send(flying[i])
            if len(out) == 2:
                results[i] = out
            else:
                flying[i] = exchange(*out)

    running = None
    for i in range(last):
        running = tiles(pos, CHUNKS[i], results[i], results[last], running)
    own, other = running
    return ((own + to_other(other)) * (1.0 / IMAGES)).T


def solution(mesh):
    axes = Mesh(mesh.devices.reshape(4, 4, 2, 4, 2), ("x", "zh", "c", "y", "zl"))
    wide, narrow = ("x", "zh", "c"), ("y", "zl")
    placed = (P(None, narrow), P(None, wide), P(narrow, wide), P(wide, narrow))
    return jax.shard_map(
        local, mesh=axes, in_specs=placed, out_specs=P(narrow, wide), check_vma=False
    )
```
